32 devices in a mesh: dp: 2 (over core), expert: 16 (over z, y, x).
Axes of the slice: x: 2, y: 2, z: 4, core: 2. Of those that a mesh axis runs over, the one named last changes fastest.
Arguments:
- queries: bfloat16 [2048, 2048], P('expert', 'dp'), may hold values from -60 to 60
- kv_cache: bfloat16 [256, 4, 128, 256], P('expert', 'dp'), may hold values from -4 to 4
- page_table: int32 [64, 4], P('expert'), may hold values from 0 to 15, as said below
- lengths: int32 [64], P('expert'), may hold values from 2 to 512, as said below
- residual: bfloat16 [2048, 2048], P('expert', 'dp'), may hold values from -0.59765625 to 0.59765625
- out_proj: bfloat16 [2048, 2048], P('dp'), may hold values from -0.125 to 0.125
- norm_gain: float32 [2048], replicated, may hold values from 0.5 to 1.5
- router: bfloat16 [2048, 64], replicated, may hold values from -0.09375 to 0.09375
- routes: int32 [2048, 6], P('expert'), may hold values from 0 to 63, all different within a row; in each aligned block of 64 rows (0 to 63, 64 to 127, ...) at most 12 rows name the same one
- placement: int32 [64, 2], replicated, may hold values from 0 to 127, as said below
- parity: int32 [64], replicated, may hold values 0 or 1
- slot_in: bfloat16 [2, 128, 2048, 2, 704], P('dp', 'expert'), may hold values from -0.125 to 0.125
- slot_out: bfloat16 [2, 128, 704, 2048], P('dp', 'expert'), may hold values from -0.625 to 0.625
- shared_in: bfloat16 [2048, 2, 1408], P(None, None, 'dp'), may hold values from -0.125 to 0.125
- shared_out: bfloat16 [1408, 2048], P('dp'), may hold values from -0.15625 to 0.15625
Outputs:
- layer_out: bfloat16 [2048, 2048], P('expert', 'dp')
The draws below stay inside these ranges and needn't reach their ends.
Inputs may be any that keep to these rules, and one draw needn't show every extreme that they name: `page_table`: rows 4 j to 4 j + 3 together hold every number of 0 to 15 once. `lengths`: entry 4 j is at least 125; each aligned group of 4 entries holds one equal to 512. `routes`: the 6 entries of a row differ; in each aligned block of 64 rows no expert is named by more than 12 rows. `placement`: its 128 entries hold every slot once.
All inputs are finite; a program needn't handle non-finite values.
Results may differ from the reference program's by a relative error of at most 0.012.
Values may be sent and summed in bfloat16 or wider, within the bound.
A program may use at most 256 MiB of HBM per device.

```python
import math
import jax
import jax.numpy as jnp
import numpy as np
from jax import lax

D = 2048
HEADS = 16
KV_HEADS = 4
HEAD_DIM = 128
EXPERTS = 64
TOP = 6
FS = 1408
PAGE = 128
ROWS_COL = 128
PRE = 125
REQ_COL = 4
BLOCK = 64
MOST = 12
MAXP = 4
POOL_COL = 16
HALF = 704
SLOTS = 128
GROUP = 128
ROWS = 2048
REQS = 64
PAGES = 256
N_DP = 2
N_EXPERT = 16


def page_helper(base_key):
    columns = REQS // REQ_COL
    subkeys = jax.random.split(base_key, columns)
    shuffled = jax.vmap(lambda subkey: jax.random.permutation(subkey, POOL_COL))(subkeys)
    return shuffled.reshape(REQS, MAXP).astype(jnp.int32)


def length_helper(base_key):
    columns = REQS // REQ_COL
    longest = MAXP * PAGE
    first_key, second_key, third_key = jax.random.split(base_key, 3)
    decoding = jax.random.randint(first_key, (columns, REQ_COL), 2, longest + 1)
    prefilling = jax.random.randint(second_key, (columns, 1), PRE, longest + 1)
    merged = jnp.concatenate([prefilling, decoding[:, 1:]], axis=1)
    chosen = jax.random.randint(third_key, (columns, 1), 0, REQ_COL)
    filled = jnp.arange(REQ_COL, dtype=jnp.int32)[None, :] == chosen
    merged = jnp.where(filled, longest, merged)
    return merged.reshape(REQS).astype(jnp.int32)


def cache_helper(base_key):
    shape = (PAGES, KV_HEADS, PAGE, 2 * HEAD_DIM)
    values = jnp.clip(jax.random.normal(base_key, shape, jnp.float32), -4.0, 4.0)
    return values


def draw_page_table(key, part):
    return page_helper(jax.random.fold_in(key, 1))


def draw_lengths(key, part):
    return length_helper(jax.random.fold_in(key, 2))


def draw_kv_cache(key, part):
    return cache_helper(jax.random.fold_in(key, 3)).astype(jnp.bfloat16)


def draw_placement(key, part):
    shuffled = jax.random.permutation(jax.random.fold_in(key, 4), 2 * EXPERTS)
    return shuffled.reshape(EXPERTS, 2).astype(jnp.int32)


def draw_queries(key, part):
    shape = (ROWS, HEADS * HEAD_DIM)
    own_key = jax.random.fold_in(key, 5)
    values = jnp.clip(jax.random.normal(own_key, shape, jnp.float32), -4.0, 4.0)
    return values.astype(jnp.bfloat16)


def with_ends(array, key, low, largest):
    longest = array.shape.index(max(array.shape))
    spots = []
    for shift in (0, 1):
        where = [jax.random.randint(jax.random.fold_in(key, axis), (), 0, length) for axis, length in enumerate(array.shape)]
        where[longest] = (where[longest] + shift) % array.shape[longest]
        spots.append(tuple(where))
    return array.at[spots[0]].set(low).at[spots[1]].set(largest)


def steps_of(stream_key, extent, cuts, low, largest):
    def one(axis_at, shards_of):
        heights = jax.random.uniform(jax.random.fold_in(jax.random.fold_in(stream_key, 6), axis_at), (shards_of,), jnp.float32, low / len(cuts), largest / len(cuts))
        return jnp.repeat(jnp.exp(heights), extent[axis_at] // shards_of).reshape((-1,) + (1,) * (len(extent) - axis_at - 1))

    loudness = one(*cuts[0])
    for cut in cuts[1:]:
        loudness = loudness * one(*cut)
    return loudness


def routed_block(key, own, number, rows, count, top, reach, lean):
    ranking = jax.random.permutation(key, count)
    packed, common = load_shares(count, rows * top, reach, lean, True), load_shares(count, rows * top, reach, lean, False)
    places = jnp.arange(count)

    def named(tallies, rotation):
        used = int((tallies > 0).sum())
        fixed = max(1, used // 4)
        moved = fixed + (places - fixed + rotation * (used - fixed)) % max(1, count - fixed)
        return jnp.zeros((count,), jnp.int32).at[ranking[jnp.where(places < fixed, places, moved)]].set(jnp.asarray(tallies, jnp.int32))

    tallies = jnp.where(number % 4 == 0, named(packed, number // 4), named(common, number - number // 4 - 1))
    mixed = jax.random.permutation(jax.random.fold_in(own, 3), count)
    giver, receiver = mixed[0:count // 2 * 2:2], mixed[1:count // 2 * 2:2]
    margin = jnp.minimum(tallies[giver] - 1, reach - tallies[receiver]) // 2
    margin = jnp.where((giver == ranking[0]) | (receiver == ranking[0]) | (tallies[receiver] == 0), 0, jnp.maximum(margin, 0))
    moved = jax.random.randint(jax.random.fold_in(own, 4), (count // 2,), 0, 1 << 20) % (margin + 1)
    tallies = tallies.at[giver].add(-moved).at[receiver].add(moved)
    items = jnp.searchsorted(jnp.cumsum(tallies), jnp.arange(rows * top), side="right").astype(jnp.int32)
    listing = items.reshape(top, rows).T
    listing = listing[jax.random.permutation(jax.random.fold_in(own, 1), rows)]
    rotation = jax.random.randint(jax.random.fold_in(own, 2), (rows, 1), 0, top)
    return jnp.take_along_axis(listing, (jnp.arange(top)[None, :] + rotation) % top, axis=1)


def load_shares(amount, total, bound, slope, full):
    portions = [(1 << 20) // math.isqrt(grade ** slope) + 1 for grade in range(1, amount + 1)]
    largest = bound if full else min(bound, max(-(-total // amount), total * portions[0] // sum(portions)))
    least = 1 if total - largest >= amount - 1 else 0
    holding, rest = [largest] + [least] * (amount - 1), total - largest - least * (amount - 1)
    while rest > 0:
        movable = [i for i in range(1, amount) if holding[i] < largest] or [i for i in range(1, amount) if holding[i] < bound]
        mass, left = sum([portions[i] for i in movable]), rest
        for i in movable:
            extra = min(bound - holding[i], max(1, left * portions[i] // mass), rest)
            holding[i] = holding[i] + extra
            rest = rest - extra
    return np.array(holding)


def gaussian(stream_key, shape, spread, reach, cuts=(), kind=jnp.bfloat16):
    drawn = spread * jax.random.normal(stream_key, shape, jnp.float32)
    if cuts:
        drawn = drawn * steps_of(stream_key, shape, cuts, -0.22, 0.18)
    return jnp.clip(drawn, -reach, reach).astype(kind)


def setup_inputs(seed: int = 0) -> dict:
    arg_keys = jax.random.split(jax.random.key(seed), 16)
    queries = draw_queries(jax.random.fold_in(arg_keys[15], 71), 0)
    kv_cache = draw_kv_cache(jax.random.fold_in(arg_keys[15], 71), 0)
    page_table = draw_page_table(jax.random.fold_in(arg_keys[15], 71), 0)
    lengths = draw_lengths(jax.random.fold_in(arg_keys[15], 71), 0)
    residual = gaussian(arg_keys[4], (ROWS, D), 0.1, 0.59765625, ((0, 16), (1, 2)))
    out_proj = gaussian(arg_keys[5], (HEADS * HEAD_DIM, D), (HEADS * HEAD_DIM) ** -0.5, 0.125, ((0, 2),))
    norm_gain = jnp.clip(1.0 + 0.1 * jax.random.normal(arg_keys[6], (D,), jnp.float32), 0.5, 1.5)
    router = gaussian(arg_keys[7], (D, EXPERTS), (2 * D) ** -0.5, 0.09375)
    routes_keys = jax.random.split(jax.random.fold_in(arg_keys[8], 1), ROWS // BLOCK)
    routes_turns = jax.random.permutation(jax.random.fold_in(arg_keys[8], 3), ROWS // BLOCK)
    routes = jax.vmap(lambda own, number: routed_block(jax.random.fold_in(arg_keys[8], 2), own, number, BLOCK, EXPERTS, TOP, MOST, 2))(routes_keys, routes_turns).reshape((ROWS, TOP))
    placement = draw_placement(jax.random.fold_in(arg_keys[15], 71), 0)
    parity = with_ends((jax.random.randint(arg_keys[10], (EXPERTS,), 0, 2) < 1).astype(jnp.int32), jax.random.fold_in(arg_keys[10], 1), 0, 1)
    slot_in = gaussian(arg_keys[11], (N_DP, GROUP, D, 2, HALF), D ** -0.5, 0.125, ((0, 2), (1, 16)))
    slot_out = gaussian(arg_keys[12], (N_DP, GROUP, HALF, D), (HALF // 8) ** -0.5, 0.625, ((0, 2), (1, 16)))
    shared_in = gaussian(arg_keys[13], (D, 2, FS), D ** -0.5, 0.125, ((2, 2),))
    shared_out = gaussian(arg_keys[14], (FS, D), FS ** -0.5, 0.15625, ((0, 2),))
    return dict(queries=queries, kv_cache=kv_cache, page_table=page_table, lengths=lengths, residual=residual, out_proj=out_proj, norm_gain=norm_gain, router=router, routes=routes, placement=placement, parity=parity, slot_in=slot_in, slot_out=slot_out, shared_in=shared_in, shared_out=shared_out)


masked_score = -1e+30
epsilon = 1e-06

def key_owners(table, first_page, pool_pages):
    request_count = table.shape[0]
    page_width = table.shape[1]
    page_ids = first_page + jnp.arange(pool_pages, dtype=jnp.int32)
    matches = (table[None, :, :] == page_ids[:, None, None]).astype(jnp.int32)
    owners = lax.optimization_barrier(jnp.sum(matches * jnp.arange(request_count, dtype=jnp.int32)[None, :, None], axis=(1, 2)))
    ordinal = lax.optimization_barrier(jnp.sum(matches * jnp.arange(page_width, dtype=jnp.int32)[None, None, :], axis=(1, 2)))
    offsets = jnp.arange(PAGE, dtype=jnp.int32)
    key_request = jnp.repeat(owners, PAGE)
    key_position = (ordinal[:, None] * PAGE + offsets[None, :]).reshape(-1)
    return (key_request, key_position)

def row_places(lengths, row_count):
    local = jnp.arange(row_count, dtype=jnp.int32)
    request = jnp.where(local < PRE, 0, local - PRE + 1).astype(jnp.int32)
    request_ids = jnp.arange(lengths.shape[0], dtype=jnp.int32)
    picked = lax.optimization_barrier(jnp.sum(jnp.where(request[:, None] == request_ids[None, :], lengths[None, :], 0), axis=1))
    position = jnp.where(local < PRE, lengths[0] - PRE + local, picked - 1).astype(jnp.int32)
    return (request, position)

def attend(queries, cache, visible):
    row_count = queries.shape[0]
    pages, local_kv, page_len, _ = cache.shape
    sharing = HEADS // KV_HEADS
    cache_float = cache.astype(jnp.float32)
    keys = cache_float[..., :HEAD_DIM]
    values = cache_float[..., HEAD_DIM:]
    query_heads = queries.reshape(row_count, local_kv, sharing, HEAD_DIM).astype(jnp.float32)
    scores = jnp.einsum('rkgd,pkod->rkgpo', query_heads, keys, precision=lax.Precision.HIGHEST)
    scores = scores.reshape(row_count, local_kv, sharing, pages * page_len) * HEAD_DIM ** (-0.5)
    allowed = visible[:, None, None, :]
    scores = jnp.where(allowed, scores, masked_score)
    highest = lax.optimization_barrier(jnp.max(scores, axis=-1))
    weights = jnp.where(allowed, jnp.exp(scores - highest[..., None]), 0.0)
    weight_sum = lax.optimization_barrier(jnp.sum(weights, axis=-1))
    rounded = lax.optimization_barrier(weights.astype(jnp.bfloat16)).astype(jnp.float32)
    rounded = rounded.reshape(row_count, local_kv, sharing, pages, page_len)
    weighted = jnp.einsum('rkgpo,pkod->rkgd', rounded, values, precision=lax.Precision.HIGHEST)
    attention = (weighted / weight_sum[..., None]).astype(jnp.bfloat16)
    return attention.reshape(row_count, local_kv * sharing * HEAD_DIM)

def route_slots(routes, placement, parity, local):
    picked = (routes[:, :, None] == jnp.arange(EXPERTS, dtype=jnp.int32)[None, None, :]).astype(jnp.int32)
    flipped = lax.optimization_barrier(jnp.sum(picked * parity[None, None, :], axis=-1))
    replica = (local[:, None] // BLOCK + flipped) % 2
    first_slot = lax.optimization_barrier(jnp.sum(picked * placement[None, None, :, 0], axis=-1))
    second_slot = lax.optimization_barrier(jnp.sum(picked * placement[None, None, :, 1], axis=-1))
    slot_ids = jnp.where(replica == 0, first_slot, second_slot).astype(jnp.int32)
    counts = lax.optimization_barrier(jnp.sum(picked, axis=1)).reshape(-1, BLOCK, EXPERTS)
    before = (jnp.cumsum(counts, axis=1) - counts).reshape(-1, EXPERTS)
    ranks = lax.optimization_barrier(jnp.sum(picked * before[:, None, :], axis=-1)).astype(jnp.int32)
    return (slot_ids, ranks)

def reference(queries, kv_cache, page_table, lengths, residual, out_proj, norm_gain, router, routes, placement, parity, slot_in, slot_out, shared_in, shared_out):
    query_groups = queries.reshape(N_EXPERT, ROWS_COL, HEADS * HEAD_DIM)
    cache_groups = kv_cache.reshape(N_EXPERT, POOL_COL, KV_HEADS, PAGE, 2 * HEAD_DIM)
    table_groups = page_table.reshape(N_EXPERT, REQ_COL, MAXP)
    length_groups = lengths.reshape(N_EXPERT, REQ_COL)

    def one_group(items):
        group_queries, group_cache, group_table, group_lengths = items
        key_request, key_position = key_owners(group_table, jnp.zeros((), jnp.int32), POOL_COL)
        request, position = row_places(group_lengths, ROWS_COL)
        visible = (key_request[None, :] == request[:, None]) & (key_position[None, :] <= position[:, None])
        return attend(group_queries, group_cache, visible)
    attention = lax.map(one_group, (query_groups, cache_groups, table_groups, length_groups)).reshape(ROWS, HEADS * HEAD_DIM)
    projected = jnp.dot(attention, out_proj, preferred_element_type=jnp.float32)
    hidden_state = (residual.astype(jnp.float32) + projected).astype(jnp.bfloat16)
    state_float = hidden_state.astype(jnp.float32)
    mean_square = lax.optimization_barrier(jnp.mean(state_float * state_float, axis=-1, keepdims=True))
    normed = (state_float * norm_gain[None, :] * lax.rsqrt(mean_square + epsilon)).astype(jnp.bfloat16)
    logits = jnp.dot(normed, router, preferred_element_type=jnp.float32)
    chosen = jnp.take_along_axis(logits, routes, axis=1)
    sigmoids = jax.nn.sigmoid(chosen)
    gates = sigmoids / lax.optimization_barrier(jnp.sum(sigmoids, axis=-1, keepdims=True))
    row_ids = jnp.arange(ROWS, dtype=jnp.int32)
    slot_ids, ranks = route_slots(routes, placement, parity, row_ids % ROWS_COL)
    source_group = (row_ids // ROWS_COL)[:, None]
    capacity = N_EXPERT * MOST
    targets = ((slot_ids * N_EXPERT + source_group) * MOST + ranks).reshape(-1)
    total_slots = SLOTS * capacity
    source = jnp.full((total_slots,), ROWS, jnp.int32).at[targets].set(jnp.broadcast_to(row_ids[:, None], slot_ids.shape).reshape(-1))
    gate_table = jnp.zeros((total_slots,), jnp.float32).at[targets].set(gates.reshape(-1))
    padded = jnp.concatenate([normed, jnp.zeros((1, D), jnp.bfloat16)], axis=0)

    def serve_slot(carry, slot_id):
        pair_index = slot_id // GROUP
        member = slot_id % GROUP
        source_rows = lax.dynamic_slice_in_dim(source, slot_id * capacity, capacity)
        row_gates = lax.dynamic_slice_in_dim(gate_table, slot_id * capacity, capacity)
        inputs = padded[source_rows]
        result = jnp.zeros((capacity, D), jnp.float32)
        for side_index in range(2):
            weights_in = slot_in[2 * pair_index + side_index, member].reshape(D, 2 * HALF)
            gate_up = jnp.dot(inputs, weights_in, preferred_element_type=jnp.float32)
            hidden_units = (jax.nn.silu(gate_up[:, :HALF]) * gate_up[:, HALF:]).astype(jnp.bfloat16)
            partial_out = jnp.dot(hidden_units, slot_out[2 * pair_index + side_index, member], preferred_element_type=jnp.float32).astype(jnp.bfloat16)
            result = result + partial_out.astype(jnp.float32)
        carry = carry.at[source_rows].add(row_gates[:, None] * result)
        return (carry, None)
    routed, _ = lax.scan(serve_slot, jnp.zeros((ROWS + 1, D), jnp.float32), jnp.arange(SLOTS, dtype=jnp.int32))
    routed = routed[:ROWS]
    shared_gate_up = jnp.dot(normed, shared_in.reshape(D, 2 * FS), preferred_element_type=jnp.float32)
    shared_hidden = (jax.nn.silu(shared_gate_up[:, :FS]) * shared_gate_up[:, FS:]).astype(jnp.bfloat16)
    shared = jnp.dot(shared_hidden, shared_out, preferred_element_type=jnp.float32)
    return (state_float + shared + routed).astype(jnp.bfloat16)
```

```python
import jax
import jax.numpy as jnp
from jax import lax
from jax.sharding import PartitionSpec as P

D = 2048
HEADS = 16
KV_HEADS = 4
HEAD_DIM = 128
EXPERTS = 64
PAGE = 128
PRE = 125
BLOCK = 64
MOST = 12


masked_score = -1e30
epsilon = 1e-06


def key_owners(table, pool_pages):
    request_count = table.shape[0]
    page_width = table.shape[1]
    page_ids = jnp.arange(pool_pages, dtype=jnp.int32)
    matches = (table[None, :, :] == page_ids[:, None, None]).astype(jnp.int32)
    owners = jnp.sum(
        matches * jnp.arange(request_count, dtype=jnp.int32)[None, :, None], axis=(1, 2)
    )
    ordinal = jnp.sum(matches * jnp.arange(page_width, dtype=jnp.int32)[None, None, :], axis=(1, 2))
    offsets = jnp.arange(PAGE, dtype=jnp.int32)
    key_request = jnp.repeat(owners, PAGE)
    key_position = (ordinal[:, None] * PAGE + offsets[None, :]).reshape(-1)
    return (key_request, key_position)


def row_places(lengths, row_count):
    local = jnp.arange(row_count, dtype=jnp.int32)
    request = jnp.where(local < PRE, 0, local - PRE + 1)
    request_ids = jnp.arange(lengths.shape[0], dtype=jnp.int32)
    picked = jnp.sum(
        jnp.where(request[:, None] == request_ids[None, :], lengths[None, :], 0), axis=1
    )
    position = jnp.where(local < PRE, lengths[0] - PRE + local, picked - 1)
    return (request, position)


def attend(queries, cache, visible):
    row_count = queries.shape[0]
    pages, local_kv, page_len, _ = cache.shape
    sharing = HEADS // KV_HEADS
    keys = cache[..., :HEAD_DIM]
    values = cache[..., HEAD_DIM:]
    query_heads = queries.reshape(row_count, local_kv, sharing, HEAD_DIM)
    scores = jnp.einsum("rkgd,pkod->rkgpo", query_heads, keys, preferred_element_type=jnp.float32)
    scores = scores.reshape(row_count, local_kv, sharing, pages * page_len) * HEAD_DIM ** (-0.5)
    allowed = visible[:, None, None, :]
    scores = jnp.where(allowed, scores, masked_score)
    highest = jnp.max(scores, axis=-1)
    weights = jnp.where(allowed, jnp.exp(scores - highest[..., None]), 0.0)
    weight_sum = jnp.sum(weights, axis=-1)
    rounded = weights.astype(jnp.bfloat16).reshape(row_count, local_kv, sharing, pages, page_len)
    weighted = jnp.einsum("rkgpo,pkod->rkgd", rounded, values, preferred_element_type=jnp.float32)
    attention = (weighted / weight_sum[..., None]).astype(jnp.bfloat16)
    return attention.reshape(row_count, local_kv * sharing * HEAD_DIM)


def route_slots(routes, placement, parity, local):
    picked = (routes[:, :, None] == jnp.arange(EXPERTS, dtype=jnp.int32)[None, None, :]).astype(
        jnp.int32
    )
    flipped = jnp.sum(picked * parity[None, None, :], axis=-1)
    replica = (local[:, None] // BLOCK + flipped) % 2
    first_slot = jnp.sum(picked * placement[None, None, :, 0], axis=-1)
    second_slot = jnp.sum(picked * placement[None, None, :, 1], axis=-1)
    slot_ids = jnp.where(replica == 0, first_slot, second_slot)
    counts = jnp.sum(picked, axis=1).reshape(-1, BLOCK, EXPERTS)
    earlier = jnp.tril(jnp.ones((BLOCK, BLOCK), jnp.bfloat16), -1)
    before = (
        jnp.einsum(
            "ts,bse->bte",
            earlier,
            counts.astype(jnp.bfloat16),
            preferred_element_type=jnp.float32,
        )
        .astype(jnp.int32)
        .reshape(-1, EXPERTS)
    )
    ranks = jnp.sum(picked * before[:, None, :], axis=-1)
    return (slot_ids, ranks)


def body(
    queries,
    kv_cache,
    page_table,
    lengths,
    residual,
    out_proj,
    norm_gain,
    router,
    routes,
    placement,
    parity,
    slot_in,
    slot_out,
    shared_in,
    shared_out,
):
    dp_count = lax.axis_size("dp")
    dp_place = lax.axis_index("dp")
    column_count = lax.axis_size("expert")
    row_count = queries.shape[0]
    pool_pages = kv_cache.shape[0]
    key_request, key_position = key_owners(page_table, pool_pages)
    request, position = row_places(lengths, row_count)
    visible = (key_request[None, :] == request[:, None]) & (
        key_position[None, :] <= position[:, None]
    )
    own_heads = attend(queries, kv_cache, visible)
    feature_width = D // dp_count
    projected = jnp.dot(own_heads, out_proj, preferred_element_type=jnp.float32)
    residual_full = lax.dynamic_update_slice(
        jnp.zeros_like(projected),
        residual.astype(jnp.float32),
        (jnp.zeros((), jnp.int32), dp_place * feature_width),
    )
    hidden_state = lax.psum(projected + residual_full, "dp").astype(jnp.bfloat16)
    state_float = hidden_state.astype(jnp.float32)
    mean_square = jnp.mean(state_float * state_float, axis=-1, keepdims=True)
    normed = (state_float * norm_gain[None, :] * lax.rsqrt(mean_square + epsilon)).astype(
        jnp.bfloat16
    )
    logits = jnp.dot(normed, router, preferred_element_type=jnp.float32)
    picked = routes[:, :, None] == jnp.arange(EXPERTS, dtype=jnp.int32)[None, None, :]
    chosen = jnp.sum(jnp.where(picked, logits[:, None, :], 0.0), axis=-1)
    sigmoids = jax.nn.sigmoid(chosen)
    gates = sigmoids / jnp.sum(sigmoids, axis=-1, keepdims=True)
    slots_here = slot_in.shape[1]
    half_units = slot_in.shape[4]
    slot_group = slots_here * column_count
    row_ids = jnp.arange(row_count, dtype=jnp.int32)
    slot_ids, ranks = route_slots(routes, placement, parity, row_ids)
    buffer_rows = slot_group * MOST
    targets = jnp.where(
        slot_ids // slot_group == dp_place // 2, slot_ids % slot_group * MOST + ranks, buffer_rows
    )
    source = (
        jnp.full((buffer_rows + 1,), row_count, jnp.int32)
        .at[targets.reshape(-1)]
        .set(jnp.broadcast_to(row_ids[:, None], targets.shape).reshape(-1))
    )
    gate_table = (
        jnp.zeros((buffer_rows + 1,), jnp.float32).at[targets.reshape(-1)].set(gates.reshape(-1))
    )
    source = source[:buffer_rows]
    gate_table = gate_table[:buffer_rows]
    padded = jnp.concatenate([normed, jnp.zeros((1, D), jnp.bfloat16)], axis=0)
    outgoing = padded[source].reshape(column_count, slots_here, MOST, D)
    weights_in = slot_in[0].reshape(slots_here, D, 2 * half_units)
    gate_up = jnp.einsum(
        "cumd,udh->cumh",
        lax.all_to_all(outgoing, "expert", split_axis=0, concat_axis=0, tiled=True),
        weights_in,
        preferred_element_type=jnp.float32,
    )
    hidden_units = (jax.nn.silu(gate_up[..., :half_units]) * gate_up[..., half_units:]).astype(
        jnp.bfloat16
    )
    returned = lax.all_to_all(
        jnp.einsum(
            "cumh,uhd->cumd", hidden_units, slot_out[0], preferred_element_type=jnp.float32
        ).astype(jnp.bfloat16),
        "expert",
        split_axis=0,
        concat_axis=0,
        tiled=True,
    )
    weighted_rows = returned.reshape(buffer_rows, D).astype(jnp.float32) * gate_table[:, None]
    routed = jax.ops.segment_sum(weighted_rows, source, num_segments=row_count + 1)[:row_count]
    shared_width = shared_in.shape[2]
    shared_gate_up = jnp.dot(
        normed, shared_in.reshape(D, 2 * shared_width), preferred_element_type=jnp.float32
    )
    shared_hidden = (
        jax.nn.silu(shared_gate_up[:, :shared_width]) * shared_gate_up[:, shared_width:]
    ).astype(jnp.bfloat16)
    shared_part = jnp.dot(shared_hidden, shared_out, preferred_element_type=jnp.float32)
    summed = lax.psum_scatter(
        (routed + shared_part).astype(jnp.bfloat16), "dp", scatter_dimension=1, tiled=True
    ).astype(jnp.float32)
    own_state = lax.dynamic_slice_in_dim(state_float, dp_place * feature_width, feature_width, 1)
    return (own_state + summed).astype(jnp.bfloat16)


def solution(mesh):
    in_specs = (
        P("expert", "dp"),
        P("expert", "dp", None, None),
        P("expert", None),
        P("expert"),
        P("expert", "dp"),
        P("dp", None),
        P(),
        P(),
        P("expert", None),
        P(),
        P(),
        P("dp", "expert", None, None, None),
        P("dp", "expert", None, None),
        P(None, None, "dp"),
        P("dp", None),
    )
    out_specs = P("expert", "dp")
    return jax.shard_map(body, mesh=mesh, in_specs=in_specs, out_specs=out_specs, check_vma=False)
```

```python
import jax
import jax.numpy as jnp
from jax import lax
from jax.sharding import PartitionSpec as P

D = 2048
HEADS = 16
KV_HEADS = 4
HEAD_DIM = 128
EXPERTS = 64
PAGE = 128
PRE = 125
BLOCK = 64
SEATS = 16


masked_score = -1e30
epsilon = 1e-06


def key_owners(table, pool_pages):
    request_count = table.shape[0]
    page_width = table.shape[1]
    page_ids = jnp.arange(pool_pages, dtype=jnp.int32)
    matches = (table[None, :, :] == page_ids[:, None, None]).astype(jnp.int32)
    owners = jnp.sum(
        matches * jnp.arange(request_count, dtype=jnp.int32)[None, :, None], axis=(1, 2)
    )
    ordinal = jnp.sum(matches * jnp.arange(page_width, dtype=jnp.int32)[None, None, :], axis=(1, 2))
    offsets = jnp.arange(PAGE, dtype=jnp.int32)
    key_request = jnp.repeat(owners, PAGE)
    key_position = (ordinal[:, None] * PAGE + offsets[None, :]).reshape(-1)
    return (key_request, key_position)


def row_places(lengths, row_count):
    local = jnp.arange(row_count, dtype=jnp.int32)
    request = jnp.where(local < PRE, 0, local - PRE + 1)
    request_ids = jnp.arange(lengths.shape[0], dtype=jnp.int32)
    picked = jnp.sum(
        jnp.where(request[:, None] == request_ids[None, :], lengths[None, :], 0), axis=1
    )
    position = jnp.where(local < PRE, lengths[0] - PRE + local, picked - 1)
    return (request, position)


def attend(queries, cache, visible):
    row_count = queries.shape[0]
    pages, local_kv, page_len, _ = cache.shape
    sharing = HEADS // KV_HEADS
    keys = cache[..., :HEAD_DIM]
    values = cache[..., HEAD_DIM:]
    query_heads = queries.reshape(row_count, local_kv, sharing, HEAD_DIM)
    scores = jnp.einsum("rkgd,pkod->rkgpo", query_heads, keys, preferred_element_type=jnp.float32)
    scores = scores.reshape(row_count, local_kv, sharing, pages * page_len) * HEAD_DIM ** (-0.5)
    allowed = visible[:, None, None, :]
    scores = jnp.where(allowed, scores, masked_score)
    highest = jnp.max(scores, axis=-1)
    weights = jnp.where(allowed, jnp.exp(scores - highest[..., None]), 0.0)
    weight_sum = jnp.sum(weights, axis=-1)
    rounded = weights.astype(jnp.bfloat16).reshape(row_count, local_kv, sharing, pages, page_len)
    weighted = jnp.einsum("rkgpo,pkod->rkgd", rounded, values, preferred_element_type=jnp.float32)
    attention = (weighted / weight_sum[..., None]).astype(jnp.bfloat16)
    return attention.reshape(row_count, local_kv * sharing * HEAD_DIM)


def slot_rows(gates, placement, parity, first_slot, slots_here):
    slot_ids = first_slot + jnp.arange(slots_here, dtype=jnp.int32)
    held = (placement[None, :, :] == slot_ids[:, None, None]).astype(jnp.int32)
    expert = jnp.sum(held * jnp.arange(EXPERTS, dtype=jnp.int32)[None, :, None], axis=(1, 2))
    side = jnp.sum(held * (jnp.arange(2, dtype=jnp.int32)[None, None, :] + parity[None, :, None]), axis=(1, 2)) % 2
    chosen = jnp.arange(EXPERTS, dtype=jnp.int32)[None, :] == expert[:, None]
    slot_gates = jnp.sum(jnp.where(chosen, gates[:, :, :, None, :], 0.0), axis=-1)
    named = slot_gates > 0.0
    halves = jnp.arange(2, dtype=jnp.int32)
    served = named & (side[None, None, None, :] == halves[None, :, None, None])
    earlier = jnp.tril(jnp.ones((BLOCK, BLOCK), jnp.bfloat16), -1)
    ranks = jnp.einsum(
        "ts,cbsu->cbtu",
        earlier,
        served.astype(jnp.bfloat16),
        preferred_element_type=jnp.float32,
    ).astype(jnp.int32)
    places = jnp.where(served, ranks, SEATS)
    places = places.reshape(places.shape[0], 2 * BLOCK, slots_here)
    slot_gates = slot_gates.reshape(places.shape)
    return jnp.swapaxes(slot_gates, 1, 2), jnp.swapaxes(places, 1, 2)


def body(
    queries,
    kv_cache,
    page_table,
    lengths,
    residual,
    out_proj,
    norm_gain,
    router,
    routes,
    placement,
    parity,
    slot_in,
    slot_out,
    shared_in,
    shared_out,
):
    dp_count = lax.axis_size("dp")
    dp_place = lax.axis_index("dp")
    column_count = lax.axis_size("expert")
    row_count = queries.shape[0]
    pool_pages = kv_cache.shape[0]
    key_request, key_position = key_owners(page_table, pool_pages)
    request, position = row_places(lengths, row_count)
    visible = (key_request[None, :] == request[:, None]) & (
        key_position[None, :] <= position[:, None]
    )
    own_heads = attend(queries, kv_cache, visible)
    feature_width = D // dp_count
    projected = jnp.dot(own_heads, out_proj, preferred_element_type=jnp.float32)
    residual_full = lax.dynamic_update_slice(
        jnp.zeros_like(projected),
        residual.astype(jnp.float32),
        (jnp.zeros((), jnp.int32), dp_place * feature_width),
    )
    hidden_state = lax.psum(projected + residual_full, "dp").astype(jnp.bfloat16)
    state_float = hidden_state.astype(jnp.float32)
    mean_square = jnp.mean(state_float * state_float, axis=-1, keepdims=True)
    normed = (state_float * norm_gain[None, :] * lax.rsqrt(mean_square + epsilon)).astype(
        jnp.bfloat16
    )
    slots_here = slot_in.shape[1]
    half_units = slot_in.shape[4]
    own_columns = lax.dynamic_slice_in_dim(normed, dp_place * feature_width, feature_width, 1)
    logits = jnp.dot(normed, router, preferred_element_type=jnp.float32)
    picked = jnp.any(
        routes[:, :, None] == jnp.arange(EXPERTS, dtype=jnp.int32)[None, None, :], axis=1
    )
    sigmoids = jnp.where(picked, jax.nn.sigmoid(logits), 0.0)
    gates = sigmoids / jnp.sum(sigmoids, axis=-1, keepdims=True)
    coarse = gates.astype(jnp.bfloat16)
    fine = (gates - coarse.astype(jnp.float32)).astype(jnp.bfloat16)
    sent = jnp.concatenate([own_columns, coarse, fine], axis=1)
    arrived = lax.all_gather(sent, "expert", axis=0)
    spread = lax.all_gather(arrived[:, :, :feature_width], "dp", axis=2, tiled=True)
    coarse = arrived[:, :, feature_width : feature_width + EXPERTS].astype(jnp.float32)
    fine = arrived[:, :, feature_width + EXPERTS :].astype(jnp.float32)
    all_gates = coarse + fine
    first_slot = lax.axis_index("expert") * slots_here
    slot_gates, places = slot_rows(
        all_gates.reshape(column_count, 2, BLOCK, -1), placement, parity, first_slot, slots_here
    )
    seat_ids = jnp.arange(SEATS, dtype=jnp.int32)
    seated = places[:, :, None, :] == seat_ids[None, None, :, None]
    moves = seated.astype(jnp.bfloat16).reshape(column_count, slots_here * SEATS, row_count)
    seat_gates = jnp.sum(jnp.where(seated, slot_gates[:, :, None, :], 0.0), axis=-1)
    seat_gates = jnp.swapaxes(seat_gates, 0, 1)
    inputs = jnp.einsum("cst,ctd->csd", moves, spread, preferred_element_type=jnp.float32).astype(
        jnp.bfloat16
    )
    inputs = jnp.swapaxes(inputs.reshape(column_count, slots_here, SEATS, D), 0, 1)
    inputs = inputs.reshape(slots_here, column_count * SEATS, D)
    gate_part = jnp.einsum(
        "usd,udh->ush", inputs, slot_in[0, :, :, 0], preferred_element_type=jnp.float32
    )
    up_part = jnp.einsum(
        "usd,udh->ush", inputs, slot_in[0, :, :, 1], preferred_element_type=jnp.float32
    )
    hidden_units = (jax.nn.silu(gate_part) * up_part).astype(jnp.bfloat16)
    results = jnp.einsum(
        "ush,uhd->usd", hidden_units, slot_out[0], preferred_element_type=jnp.float32
    )
    weighted = (results * seat_gates.reshape(slots_here, -1)[:, :, None]).astype(jnp.bfloat16)
    weighted = jnp.swapaxes(weighted.reshape(slots_here, column_count, SEATS, D), 0, 1)
    weighted = weighted.reshape(column_count, slots_here * SEATS, D)
    shared_gate = jnp.dot(normed, shared_in[:, 0], preferred_element_type=jnp.float32)
    shared_up = jnp.dot(normed, shared_in[:, 1], preferred_element_type=jnp.float32)
    shared_hidden = (jax.nn.silu(shared_gate) * shared_up).astype(jnp.bfloat16)
    shared_part = jnp.dot(shared_hidden, shared_out, preferred_element_type=jnp.float32)
    shared_sum = lax.psum_scatter(
        shared_part.astype(jnp.bfloat16), "dp", scatter_dimension=1, tiled=True
    ).astype(jnp.float32)
    partial = jnp.einsum("cst,csd->ctd", moves, weighted, preferred_element_type=jnp.float32)
    partial = partial.astype(jnp.bfloat16).reshape(column_count * row_count, D)
    chip = lax.psum_scatter(partial, "dp", scatter_dimension=1, tiled=True)
    routed = lax.psum_scatter(chip, "expert", scatter_dimension=0, tiled=True)
    summed = routed.astype(jnp.float32) + shared_sum
    own_state = lax.dynamic_slice_in_dim(state_float, dp_place * feature_width, feature_width, 1)
    return (own_state + summed).astype(jnp.bfloat16)


def solution(mesh):
    in_specs = (
        P("expert", "dp"),
        P("expert", "dp", None, None),
        P("expert", None),
        P("expert"),
        P("expert", "dp"),
        P("dp", None),
        P(),
        P(),
        P("expert", None),
        P(),
        P(),
        P("dp", "expert", None, None, None),
        P("dp", "expert", None, None),
        P(None, None, "dp"),
        P("dp", None),
    )
    out_specs = P("expert", "dp")
    return jax.shard_map(body, mesh=mesh, in_specs=in_specs, out_specs=out_specs, check_vma=False)
```
